32 devices in a mesh: exp: 4 (over y, x), fsdp: 8 (over z, core).
Axes of the slice: x: 2, y: 2, z: 4, core: 2. Of those that a mesh axis runs over, the one named last changes fastest.
Arguments:
- tokens: bfloat16 [1024, 3072], P('fsdp'), may hold values from -6 to 6
- out_grad: bfloat16 [1024, 3072], P('fsdp'), may hold values from -6 to 6
- experts_chosen: int32 [1024, 2], P('fsdp'), may hold values from 0 to 3, all different within a row; in each aligned block of 128 rows (0 to 127, 128 to 255, ...) at most 80 rows name the same one
- route_weight: float32 [1024, 2], P('fsdp'), may hold values from 0.1 to 0.9
- w_gate: bfloat16 [4, 3072, 8192], P('exp', None, 'fsdp'), may hold values from -0.109375 to 0.109375
- w_up: bfloat16 [4, 3072, 8192], P('exp', None, 'fsdp'), may hold values from -0.109375 to 0.109375
- w_down: bfloat16 [4, 8192, 3072], P('exp', 'fsdp'), may hold values from -0.0625 to 0.0625
- projection: bfloat16 [512, 3072], P(None, 'fsdp'), may hold values from -0.109375 to 0.109375
- mom_gate: float32 [4, 512, 8192], P('exp', None, 'fsdp'), may hold values from -3 to 3
- mom_up: float32 [4, 512, 8192], P('exp', None, 'fsdp'), may hold values from -3 to 3
- mom_down: float32 [4, 8192, 512], P('exp', 'fsdp'), may hold values from -3 to 3
Outputs:
- grad_tokens: bfloat16 [1024, 3072], P('fsdp')
- new_gate_mom: float32 [4, 512, 8192], P('exp', None, 'fsdp')
- new_up_mom: float32 [4, 512, 8192], P('exp', None, 'fsdp')
- new_down_mom: float32 [4, 8192, 512], P('exp', 'fsdp')
The draws below stay inside these ranges and needn't reach their ends.
Inputs may be any that keep to these rules, and one draw needn't show every extreme that they name: `experts_chosen`: each row names 2 different experts. In each aligned block of 128 rows no expert is named by more than 80 rows, a bound that some block reaches.
All inputs are finite; a program needn't handle non-finite values.
Results may differ from the reference program's by a relative error of at most 0.015.
Values may be sent and summed in bfloat16 or wider, within the bound.
No kernel may reach another device: no remote copies, remote signals or barrier semaphores. Data moves between devices by JAX's collectives and lax.ppermute only.
A program may use at most 128 MiB of HBM per device.

```python
import math
import jax
import jax.numpy as jnp
import numpy as np
from jax import lax

D = 3072
FF = 8192
EXPERTS = 4
TOP = 2
RANK = 512
TOK_DEV = 128
TOKENS = 1024
CAP = 80
N_FSDP = 8


def level_of(own_key, extent, pieces, least, high):
    gain, own = 1.0, jax.random.fold_in(own_key, 6)
    for dim, parts in pieces:
        steps = jnp.exp(jax.random.uniform(jax.random.fold_in(own, dim), (parts,), jnp.float32, least / len(pieces), high / len(pieces)))
        gain = gain * jnp.repeat(steps, extent[dim] // parts).reshape([-1 if axis == dim else 1 for axis in range(len(extent))])
    return gain


def assign_block(rng, own, number, rows, amount, top, reach, slope):
    order = jax.random.permutation(rng, amount)
    heavy_load, usual = load_shares(amount, rows * top, reach, slope, True), load_shares(amount, rows * top, reach, slope, False)
    places = jnp.arange(amount)

    def named(tallies, turn):
        used = int((tallies > 0).sum())
        fixed = max(1, used // 4)
        moved = fixed + (places - fixed + turn * (used - fixed)) % max(1, amount - fixed)
        return jnp.zeros((amount,), jnp.int32).at[order[jnp.where(places < fixed, places, moved)]].set(jnp.asarray(tallies, jnp.int32))

    tallies = jnp.where(number % 4 == 0, named(heavy_load, number // 4), named(usual, number - number // 4 - 1))
    mixed = jax.random.permutation(jax.random.fold_in(own, 3), amount)
    donor, receiver = mixed[0:amount // 2 * 2:2], mixed[1:amount // 2 * 2:2]
    slack = jnp.minimum(tallies[donor] - 1, reach - tallies[receiver]) // 2
    slack = jnp.where((donor == order[0]) | (receiver == order[0]) | (tallies[receiver] == 0), 0, jnp.maximum(slack, 0))
    moved = jax.random.randint(jax.random.fold_in(own, 4), (amount // 2,), 0, 1 << 20) % (slack + 1)
    tallies = tallies.at[donor].add(-moved).at[receiver].add(moved)
    members = jnp.searchsorted(jnp.cumsum(tallies), jnp.arange(rows * top), side="right").astype(jnp.int32)
    grid = members.reshape(top, rows).T
    grid = grid[jax.random.permutation(jax.random.fold_in(own, 1), rows)]
    turn = jax.random.randint(jax.random.fold_in(own, 2), (rows, 1), 0, top)
    return jnp.take_along_axis(grid, (jnp.arange(top)[None, :] + turn) % top, axis=1)


def load_shares(number_of, total, limit, skew, full):
    weights = [(1 << 20) // math.isqrt(rank ** skew) + 1 for rank in range(1, number_of + 1)]
    largest = limit if full else min(limit, max(-(-total // number_of), total * weights[0] // sum(weights)))
    least = 1 if total - largest >= number_of - 1 else 0
    holding, rest = [largest] + [least] * (number_of - 1), total - largest - least * (number_of - 1)
    while rest > 0:
        candidates = [i for i in range(1, number_of) if holding[i] < largest] or [i for i in range(1, number_of) if holding[i] < limit]
        mass, remaining = sum([weights[i] for i in candidates]), rest
        for i in candidates:
            extra = min(limit - holding[i], max(1, remaining * weights[i] // mass), rest)
            holding[i] = holding[i] + extra
            rest = rest - extra
    return np.array(holding)


def gaussian(own_key, shape, deviation, most, cuts=(), held_as=jnp.bfloat16):
    result = deviation * jax.random.normal(own_key, shape, jnp.float32)
    if cuts:
        result = result * level_of(own_key, shape, cuts, -0.22, 0.18)
    return jnp.clip(result, -most, most).astype(held_as)


def setup_inputs(seed: int = 0) -> dict:
    streams_of = jax.random.split(jax.random.key(seed), 12)
    tokens = gaussian(streams_of[0], (TOKENS, D), 1.0, 6.0, ((0, 8),))
    out_grad = gaussian(streams_of[1], (TOKENS, D), 1.0, 6.0, ((0, 8),))
    experts_chosen_keys = jax.random.split(jax.random.fold_in(streams_of[2], 1), TOKENS // TOK_DEV)
    experts_chosen_turns = jax.random.permutation(jax.random.fold_in(streams_of[2], 3), TOKENS // TOK_DEV)
    experts_chosen = jax.vmap(lambda own, number: assign_block(jax.random.fold_in(streams_of[2], 2), own, number, TOK_DEV, EXPERTS, TOP, CAP, 2))(experts_chosen_keys, experts_chosen_turns).reshape((TOKENS, TOP))
    route_weight = jnp.clip(0.1 + 0.79999997 * jax.random.uniform(streams_of[3], (TOKENS, TOP), jnp.float32) ** level_of(streams_of[3], (TOKENS, TOP), ((0, 8),), -0.2, 0.2), 0.1, 0.9)
    w_gate = gaussian(streams_of[4], (EXPERTS, D, FF), D ** -0.5, 0.109375, ((0, 4), (2, 8)))
    w_up = gaussian(streams_of[5], (EXPERTS, D, FF), D ** -0.5, 0.109375, ((0, 4), (2, 8)))
    w_down = gaussian(streams_of[6], (EXPERTS, FF, D), FF ** -0.5, 0.0625, ((0, 4), (1, 8)))
    projection = gaussian(streams_of[7], (RANK, D), D ** -0.5, 0.109375, ((1, 8),))
    mom_gate = gaussian(streams_of[8], (EXPERTS, RANK, FF), 0.5, 3.0, ((0, 4), (2, 8)), jnp.float32)
    mom_up = gaussian(streams_of[9], (EXPERTS, RANK, FF), 0.5, 3.0, ((0, 4), (2, 8)), jnp.float32)
    mom_down = gaussian(streams_of[10], (EXPERTS, FF, RANK), 0.5, 3.0, ((0, 4), (1, 8)), jnp.float32)
    return {"tokens": tokens, "out_grad": out_grad, "experts_chosen": experts_chosen, "route_weight": route_weight, "w_gate": w_gate, "w_up": w_up, "w_down": w_down, "projection": projection, "mom_gate": mom_gate, "mom_up": mom_up, "mom_down": mom_down}


momentum_decay = 0.9
grad_share = 0.1


def rounded(value):
    return lax.optimization_barrier(value.astype(jnp.bfloat16)).astype(jnp.float32)


def contract_last(left, right):
    return lax.dot_general(left, right, (((1,), (1,)), ((), ())), preferred_element_type=jnp.float32)


def contract_first(left, right):
    return lax.dot_general(left, right, (((0,), (0,)), ((), ())), preferred_element_type=jnp.float32)


def reference(tokens, out_grad, experts_chosen, route_weight, w_gate, w_up, w_down, projection, mom_gate, mom_up, mom_down):
    chosen_blocks = experts_chosen.reshape(N_FSDP, TOK_DEV, TOP)
    weight_blocks = route_weight.reshape(N_FSDP, TOK_DEV, TOP)
    token_blocks = tokens.astype(jnp.float32).reshape(N_FSDP, TOK_DEV, D)
    grad_blocks = out_grad.astype(jnp.float32).reshape(N_FSDP, TOK_DEV, D)
    places = jnp.arange(CAP, dtype=jnp.int32)
    block_ids = jnp.arange(N_FSDP, dtype=jnp.int32)
    width_block = FF // N_FSDP
    total = jnp.zeros((N_FSDP, TOK_DEV, D), jnp.float32)
    gate_moms = []
    up_moms = []
    down_moms = []
    for expert in range(EXPERTS):
        hit = chosen_blocks == expert
        member = jnp.any(hit, axis=2).astype(jnp.int32)
        route = jnp.sum(jnp.where(hit, weight_blocks, jnp.zeros_like(weight_blocks)), axis=2)
        slot_pos = jnp.cumsum(member, axis=1, dtype=jnp.int32) - 1
        select_mat = ((slot_pos[:, None, :] == places[None, :, None]) & (member[:, None, :] > 0)).astype(jnp.float32)
        scaled = rounded(route[:, :, None] * grad_blocks)
        x_rows = jnp.einsum("fct,ftd->fcd", select_mat, token_blocks, precision=lax.Precision.HIGHEST)
        x_rows = x_rows.reshape(N_FSDP * CAP, D).astype(jnp.bfloat16)
        grad_rows = jnp.einsum("fct,ftd->fcd", select_mat, scaled, precision=lax.Precision.HIGHEST)
        grad_rows = grad_rows.reshape(N_FSDP * CAP, D).astype(jnp.bfloat16)
        gate_weight = w_gate[expert]
        up_weight = w_up[expert]
        gate = jnp.dot(x_rows, gate_weight, preferred_element_type=jnp.float32)
        up = jnp.dot(x_rows, up_weight, preferred_element_type=jnp.float32)
        sigma = jax.nn.sigmoid(gate)
        silu = gate * sigma
        hidden = (silu * up).astype(jnp.bfloat16)
        back = contract_last(grad_rows, w_down[expert])
        d_gate = (back * up * sigma * (1.0 + gate * (1.0 - sigma))).astype(jnp.bfloat16)
        d_up = (back * silu).astype(jnp.bfloat16)

        def add_block(accum, index):
            start = index * width_block
            term = contract_last(lax.dynamic_slice_in_dim(d_gate, start, width_block, 1),
                                 lax.dynamic_slice_in_dim(gate_weight, start, width_block, 1))
            term = term + contract_last(lax.dynamic_slice_in_dim(d_up, start, width_block, 1),
                                        lax.dynamic_slice_in_dim(up_weight, start, width_block, 1))
            return accum + rounded(term), index

        row_grad, unused = lax.scan(add_block, jnp.zeros((N_FSDP * CAP, D), jnp.float32), block_ids)
        total = total + jnp.einsum("fct,fcd->ftd", select_mat, row_grad.reshape(N_FSDP, CAP, D),
                                   precision=lax.Precision.HIGHEST)
        low_tokens = contract_last(x_rows, projection).astype(jnp.bfloat16)
        low_grad = contract_last(grad_rows, projection).astype(jnp.bfloat16)
        gate_moms.append(momentum_decay * mom_gate[expert] + grad_share * contract_first(low_tokens, d_gate))
        up_moms.append(momentum_decay * mom_up[expert] + grad_share * contract_first(low_tokens, d_up))
        down_moms.append(momentum_decay * mom_down[expert] + grad_share * contract_first(hidden, low_grad))
    grad_tokens = total.reshape(N_FSDP * TOK_DEV, D).astype(jnp.bfloat16)
    return (grad_tokens, jnp.stack(gate_moms), jnp.stack(up_moms), jnp.stack(down_moms))
```

```python
import jax
import jax.numpy as jnp
from jax import lax
from jax.sharding import PartitionSpec as P

momentum_decay = 0.9
grad_share = 0.1
parts_of_quarter = 2


def contract_last(left, right):
    return lax.dot_general(
        left, right, (((1,), (1,)), ((), ())), preferred_element_type=jnp.float32
    )


def contract_first(left, right):
    return lax.dot_general(
        left, right, (((0,), (0,)), ((), ())), preferred_element_type=jnp.float32
    )


def plane_swap(array, step, count):
    return lax.ppermute(array, "exp", [(i, i ^ step) for i in range(count)])


def core_swap(array, count):
    return lax.ppermute(array, "fsdp", [(i, i ^ 1) for i in range(count)])


def chip_shift(array, step, count):
    return lax.ppermute(array, "fsdp", [(i, (i + 2 * step) % count) for i in range(count)])


def routing_rows(experts_chosen, route_weight):
    rows = [experts_chosen.astype(jnp.float32).T]
    rest = route_weight.T
    for unused in range(3):
        term = lax.reduce_precision(rest, 8, 7)
        rows.append(term)
        rest = rest - term
    return jnp.concatenate(rows, axis=0).astype(jnp.bfloat16)


def read_routing(rows, experts, capacity):
    blocks, tall, tok_count = rows.shape
    top = tall // 4
    values = rows.astype(jnp.float32)
    chosen = values[:, :top]
    weight = values[:, top : 2 * top] + values[:, 2 * top : 3 * top] + values[:, 3 * top :]
    hit = chosen[:, None] == experts.astype(jnp.float32)[None, :, None, None]
    member = jnp.any(hit, axis=2)
    route = jnp.sum(jnp.where(hit, weight[:, None], 0.0), axis=2)
    before = lax.broadcasted_iota(jnp.int32, (tok_count, tok_count), 0)
    after = lax.broadcasted_iota(jnp.int32, (tok_count, tok_count), 1)
    slot = jnp.dot(
        member.astype(jnp.bfloat16).reshape(-1, tok_count),
        (before < after).astype(jnp.bfloat16),
        preferred_element_type=jnp.float32,
    ).reshape(member.shape)
    places = lax.broadcasted_iota(jnp.int32, (capacity, tok_count), 0).astype(jnp.float32)
    select = (slot[:, :, None, :] == places) & member[:, :, None, :]
    route_rows = jnp.sum(jnp.where(select, route[:, :, None, :], 0.0), axis=3)
    return select.astype(jnp.bfloat16), route_rows


def shards(
    tokens,
    out_grad,
    experts_chosen,
    route_weight,
    w_gate,
    w_up,
    w_down,
    projection,
    mom_gate,
    mom_up,
    mom_down,
):
    tok_count, width = tokens.shape
    top_count = experts_chosen.shape[1]
    count_exp = lax.axis_size("exp")
    count_fsdp = lax.axis_size("fsdp")
    chips = count_fsdp // 2
    experts_all = count_exp * w_gate.shape[0]
    capacity = min(tok_count, tok_count * top_count * 5 // (4 * experts_all))
    quarter = width // count_exp
    expert = lax.axis_index("exp")
    gate_weight = w_gate[0]
    up_weight = w_up[0]
    down_weight = w_down[0]
    bf16 = jnp.bfloat16

    steps = range(1, chips)
    own_routing = routing_rows(experts_chosen, route_weight)
    tall = own_routing.shape[0]
    start = expert * quarter
    x_part = lax.dynamic_slice_in_dim(tokens, start, quarter, 1)
    x_part = jnp.concatenate(
        [x_part, jnp.pad(own_routing, ((0, 0), (0, quarter - tok_count)))], axis=0
    )
    g_part = lax.dynamic_slice_in_dim(out_grad, start, quarter, 1)
    x_got = [chip_shift(x_part, k, count_fsdp) for k in steps]
    g_part, x_got = lax.optimization_barrier((g_part, x_got))
    g_got = [chip_shift(g_part, k, count_fsdp) for k in steps]

    order = expert ^ jnp.arange(count_exp, dtype=jnp.int32)
    rows = jnp.stack([own_routing] + [a[tok_count:, :tok_count] for a in x_got])
    select, route_rows = read_routing(rows, order, capacity)

    def pick(sel, array):
        return jnp.dot(sel, array, preferred_element_type=jnp.float32)

    def spread(whole, got, scale):
        sends = []
        for k in steps:
            picked = pick(select[k].reshape(count_exp * capacity, tok_count), got[k - 1])
            if scale:
                picked = picked * route_rows[k].reshape(-1, 1)
            sends.append(picked.astype(bf16).reshape(count_exp, capacity, quarter))
        sends = jnp.stack(sends, axis=1).reshape(count_exp, (chips - 1) * capacity, quarter)
        own = pick(select[0, 0], whole)
        if scale:
            own = own * route_rows[0, 0][:, None]
        far = jnp.zeros(((chips - 1) * capacity, width), bf16)
        for m in range(count_exp):
            piece = sends[m] if m == 0 else plane_swap(sends[m], m, count_exp)
            far = lax.dynamic_update_slice(far, piece, (0, (expert ^ m) * quarter))
        return jnp.concatenate([own.astype(bf16), far], axis=0)

    x_mine = spread(tokens, [a[:tok_count] for a in x_got], False)
    x_other = core_swap(x_mine, count_fsdp)
    grad_mine = spread(out_grad, g_got, True)
    grad_other = core_swap(grad_mine, count_fsdp)
    projection, unused = lax.optimization_barrier((projection, x_mine))
    proj_full = lax.all_gather(projection, "fsdp", axis=1, tiled=True)

    x_all = jnp.concatenate([x_mine, x_other], axis=0)
    grad_all = jnp.concatenate([grad_mine, grad_other], axis=0)
    half = chips * capacity
    gate = jnp.dot(x_all, gate_weight, preferred_element_type=jnp.float32)
    up = jnp.dot(x_all, up_weight, preferred_element_type=jnp.float32)
    sigma = jax.nn.sigmoid(gate)
    silu = gate * sigma
    hidden = (silu * up).astype(bf16)
    bwd_out = contract_last(grad_all, down_weight)
    d_gate = (bwd_out * up * sigma * (1.0 + gate * (1.0 - sigma))).astype(bf16)
    d_up = (bwd_out * silu).astype(bf16)

    sub = quarter // parts_of_quarter
    pieces = []
    for h in range(parts_of_quarter):

        def rows_of(weight):
            return weight.reshape(count_exp, parts_of_quarter, sub, -1)[:, h].reshape(
                count_exp * sub, -1
            )

        part = (
            contract_last(d_gate, rows_of(gate_weight)) + contract_last(d_up, rows_of(up_weight))
        ).astype(bf16)
        from_core = core_swap(part[half:], count_fsdp)
        summed = (part[:half].astype(jnp.float32) + from_core.astype(jnp.float32)).astype(bf16)
        came = []
        for m in range(count_exp):
            piece = lax.dynamic_slice_in_dim(summed, (expert ^ m) * sub, sub, 1)
            if m:
                piece = plane_swap(piece, m, count_exp)
            came.append(piece.reshape(chips, capacity, sub))
        came = jnp.stack(came, axis=1).reshape(chips, count_exp * capacity, sub)
        total = jnp.zeros((tok_count, sub), jnp.float32)
        for k in range(chips):
            back = contract_first(select[k].reshape(count_exp * capacity, tok_count), came[k])
            if k:
                back = chip_shift(back.astype(bf16), chips - k, count_fsdp).astype(jnp.float32)
            total = total + back
        pieces.append(total.astype(bf16))

    grad_tokens = jnp.zeros((tok_count, width), bf16)
    for h, piece in enumerate(pieces):
        for m in range(count_exp):
            got = piece if m == 0 else plane_swap(piece, m, count_exp)
            grad_tokens = lax.dynamic_update_slice(
                grad_tokens, got, (0, (expert ^ m) * quarter + h * sub)
            )

    low_tokens = contract_last(x_all, proj_full).astype(bf16)
    low_grad = contract_last(grad_all, proj_full).astype(bf16)
    new_gate = momentum_decay * mom_gate + grad_share * contract_first(low_tokens, d_gate)[None]
    new_up = momentum_decay * mom_up + grad_share * contract_first(low_tokens, d_up)[None]
    new_down = momentum_decay * mom_down + grad_share * contract_first(hidden, low_grad)[None]
    return (grad_tokens, new_gate, new_up, new_down)


def solution(mesh):
    in_specs = (
        P("fsdp", None),
        P("fsdp", None),
        P("fsdp", None),
        P("fsdp", None),
        P("exp", None, "fsdp"),
        P("exp", None, "fsdp"),
        P("exp", "fsdp", None),
        P(None, "fsdp"),
        P("exp", None, "fsdp"),
        P("exp", None, "fsdp"),
        P("exp", "fsdp", None),
    )
    out_specs = (
        P("fsdp", None),
        P("exp", None, "fsdp"),
        P("exp", None, "fsdp"),
        P("exp", "fsdp", None),
    )
    return jax.shard_map(shards, mesh=mesh, in_specs=in_specs, out_specs=out_specs, check_vma=False)
```

```python
import functools

import jax
import jax.numpy as jnp
from jax import lax
from jax.experimental import pallas as pl
from jax.experimental.pallas import tpu as pltpu
from jax.sharding import PartitionSpec as P

momentum_decay = 0.9
grad_share = 0.1
lanes = 128
bf16 = jnp.bfloat16
f32 = jnp.float32
vmem = pl.BlockSpec(memory_space=pltpu.VMEM)
smem = pl.BlockSpec(memory_space=pltpu.SMEM)


def contract_last(left, right):
    return lax.dot_general(left, right, (((1,), (1,)), ((), ())), preferred_element_type=f32)


def contract_first(left, right):
    return lax.dot_general(left, right, (((0,), (0,)), ((), ())), preferred_element_type=f32)


def plain(left, right):
    return jnp.dot(left, right, preferred_element_type=f32)


def plane_swap(array, step, count):
    return lax.ppermute(array, "exp", [(i, i ^ step) for i in range(count)])


def core_swap(array, count):
    return lax.ppermute(array, "fsdp", [(i, i ^ 1) for i in range(count)])


def after(value, *others):
    return lax.optimization_barrier((value, others))[0]


def chip_swap(array, step, count):
    return lax.ppermute(array, "fsdp", [(i, i ^ (2 * step)) for i in range(count)])


def tile_of(size, wanted):
    return wanted if size % wanted == 0 else size


def routing_rows(experts_chosen, route_weight):
    rows = [experts_chosen.astype(f32).T]
    rest = route_weight.T
    for unused in range(3):
        term = lax.reduce_precision(rest, 8, 7)
        rows.append(term)
        rest = rest - term
    rows = jnp.concatenate(rows, axis=0)
    return jnp.pad(rows, ((0, -rows.shape[0] % 16), (0, 0))).astype(bf16)


def select_kernel(top, ids, own, *refs):
    experts = ids.shape[0]
    blocks = len(refs) - 1 - experts
    got, sends = refs[: blocks - 1], refs[blocks - 1 : blocks - 1 + experts]
    select, route_rows = refs[-2:]
    tok_count = own.shape[1]
    capacity = select.shape[1] // experts
    below = lax.broadcasted_iota(jnp.int32, (tok_count, tok_count), 0)
    right = lax.broadcasted_iota(jnp.int32, (tok_count, tok_count), 1)
    earlier = (below < right).astype(f32).astype(bf16)
    places = lax.broadcasted_iota(jnp.int32, (capacity, tok_count), 0).astype(f32)
    for k in range(blocks):
        rows = (own[...] if k == 0 else got[k - 1][tok_count : tok_count + own.shape[0], :tok_count]).astype(f32)
        chosen = rows[:top]
        weight = rows[top : 2 * top] + rows[2 * top : 3 * top] + rows[3 * top : 4 * top]
        members, routes = [], []
        for m in range(experts):
            hit = (chosen == ids[m].astype(f32)).astype(f32)
            members.append(jnp.max(hit, axis=0, keepdims=True))
            routes.append(jnp.sum(hit * weight, axis=0, keepdims=True))
        member = jnp.concatenate(members, axis=0)
        slot = plain(member.astype(bf16), earlier)
        for m in range(experts):
            here = (slot[m : m + 1] == places) & (member[m : m + 1] > 0.0)
            one = here.astype(f32)
            select[k, m * capacity : (m + 1) * capacity, :] = one.astype(bf16)
            share = jnp.sum(one * routes[m], axis=1, keepdims=True)
            route_rows[k, m * capacity : (m + 1) * capacity, :] = jnp.broadcast_to(
                share, (capacity, lanes)
            )
            if k:
                sends[m][(k - 1) * capacity : k * capacity, :] = plain(
                    one.astype(bf16), got[k - 1][:tok_count, :]
                ).astype(bf16)


def scaled_kernel(select, route_rows, *refs):
    blocks = select.shape[0]
    got, sends = refs[: blocks - 1], refs[blocks - 1 :]
    capacity = select.shape[1] // len(sends)
    for k in range(1, blocks):
        for m in range(len(sends)):
            span = slice(m * capacity, (m + 1) * capacity)
            rows = plain(select[k, span, :], got[k - 1][...]) * route_rows[k, span, :1]
            sends[m][(k - 1) * capacity : k * capacity, :] = rows.astype(bf16)


def pack_kernel(scale, starts, select, route_rows, whole, *refs):
    pieces, out = refs[:-1], refs[-1]
    experts = len(pieces)
    capacity = select.shape[1] // experts
    quarter = pieces[0].shape[1]
    own = plain(select[0, :capacity, :], whole[...])
    if scale:
        own = own * route_rows[0, :capacity, :1]
    out[:capacity, :] = own.astype(bf16)
    for m in range(experts):
        columns = pl.ds(pl.multiple_of(starts[m], lanes), quarter)
        out[capacity:, columns] = pieces[m][...]


def forward_kernel(mine, other, w_gate, w_up, *outs):
    for half, rows in enumerate((mine, other)):
        hidden, silu_out, factor_out = outs[3 * half : 3 * half + 3]
        gate = plain(rows[...], w_gate[0])
        up = plain(rows[...], w_up[0])
        sigma = jax.nn.sigmoid(gate)
        silu = gate * sigma
        hidden[...] = (silu * up).astype(bf16)
        silu_out[...] = silu.astype(bf16)
        factor_out[...] = (up * sigma * (1.0 + gate * (1.0 - sigma))).astype(bf16)


def back_kernel(grad, w_down, silu, factor, *refs):
    d_gate, d_up = refs[-2:]
    back = contract_last(grad[...], w_down[0])
    d_gate[...] = (back * factor[...].astype(f32)).astype(bf16)
    d_up[...] = (back * silu[...].astype(f32)).astype(bf16)


def merge_kernel(starts, part, more, *outs):
    half, sub = outs[0].shape
    for m, out in enumerate(outs):
        columns = pl.ds(pl.multiple_of(starts[m], lanes), sub)
        out[...] = (part[:half, columns].astype(f32) + more[:, columns].astype(f32)).astype(bf16)


def place_kernel(starts, *refs):
    pieces, out = refs[:-1], refs[-1]
    experts = starts.shape[0]
    sub = pieces[0].shape[1]
    for i, piece in enumerate(pieces):
        first = starts[i % experts] + (i // experts) * experts * sub
        out[:, pl.ds(pl.multiple_of(first, lanes), sub)] = piece[...]


def token_kernel(select, *refs):
    blocks = select.shape[0]
    came, outs = refs[:-blocks], refs[-blocks:]
    capacity = select.shape[1] // len(came)
    for k in range(blocks):
        rows = jnp.concatenate(
            [piece[k * capacity : (k + 1) * capacity, :] for piece in came], axis=0
        )
        outs[k][...] = contract_first(select[k], rows).astype(outs[k].dtype)


def low_kernel(mine, other, g_mine, g_other, projection, *outs):
    for rows, out in zip((mine, other, g_mine, g_other), outs):
        out[...] = contract_last(rows[...], projection[...]).astype(bf16)


def momentum_kernel(lt0, lt1, lg0, lg1, d_gate, d_up, h0, h1, mg, mu, md, og, ou, od):
    half = lt0.shape[0]
    for old, new, pairs in (
        (mg, og, ((lt0[...], d_gate[:half, :]), (lt1[...], d_gate[half:, :]))),
        (mu, ou, ((lt0[...], d_up[:half, :]), (lt1[...], d_up[half:, :]))),
        (md, od, ((h0[...], lg0[...]), (h1[...], lg1[...]))),
    ):
        total = contract_first(*pairs[0]) + contract_first(*pairs[1])
        new[0] = momentum_decay * old[0] + grad_share * total


def call(
    kernel, name, shapes, in_specs, out_specs, grid=(), scalars=0, limit=16, alias=None, flops=0
):
    return pl.pallas_call(
        kernel,
        name=name,
        out_shape=[jax.ShapeDtypeStruct(s, t) for s, t in shapes],
        grid_spec=pltpu.PrefetchScalarGridSpec(
            num_scalar_prefetch=scalars, grid=grid, in_specs=in_specs, out_specs=out_specs
        ),
        input_output_aliases=alias or {},
        compiler_params=pltpu.CompilerParams(vmem_limit_bytes=limit << 20),
        cost_estimate=pl.CostEstimate(flops=flops, bytes_accessed=0, transcendentals=0),
    )


def shards(
    tokens,
    out_grad,
    experts_chosen,
    route_weight,
    w_gate,
    w_up,
    w_down,
    projection,
    mom_gate,
    mom_up,
    mom_down,
):
    tok_count, width = tokens.shape
    top = experts_chosen.shape[1]
    hidden_local = w_gate.shape[2]
    rank = projection.shape[0]
    count_exp = lax.axis_size("exp")
    count_fsdp = lax.axis_size("fsdp")
    chips = count_fsdp // 2
    experts_all = count_exp * w_gate.shape[0]
    capacity = min(tok_count, tok_count * top * 5 // (4 * experts_all))
    capacity = -(-capacity // 16) * 16
    quarter = width // count_exp
    half = chips * capacity
    far = (chips - 1) * capacity
    expert = lax.axis_index("exp")
    steps = range(1, chips)
    order = expert ^ jnp.arange(count_exp, dtype=jnp.int32)
    starts = order * quarter

    own_routing = routing_rows(experts_chosen, route_weight)
    tall = own_routing.shape[0]
    start = expert * quarter
    x_part = jnp.concatenate(
        [
            lax.dynamic_slice_in_dim(tokens, start, quarter, 1),
            jnp.pad(own_routing, ((0, 0), (0, quarter - tok_count))),
        ],
        axis=0,
    )
    g_part = lax.dynamic_slice_in_dim(out_grad, start, quarter, 1)
    x_got = [chip_swap(x_part, k, count_fsdp) for k in steps]
    g_part = after(g_part, x_got)
    g_got = [chip_swap(g_part, k, count_fsdp) for k in steps]

    parts_of_quarter = next(n for n in (2, 3, 1) if quarter % (n * lanes) == 0 or n == 1)
    sub = quarter // parts_of_quarter

    send_shapes = [((far, quarter), bf16)] * count_exp
    *x_send, select, route_rows = call(
        functools.partial(select_kernel, top),
        "select",
        send_shapes
        + [
            ((chips, count_exp * capacity, tok_count), bf16),
            ((chips, count_exp * capacity, lanes), f32),
        ],
        [smem] + [vmem] * chips,
        [vmem] * (count_exp + 2),
    )(order, own_routing, *x_got)

    def gathered(send):
        return [send[0]] + [plane_swap(send[m], m, count_exp) for m in range(1, count_exp)]

    def pack(scale, whole, pieces):
        return call(
            functools.partial(pack_kernel, scale),
            "pack",
            [((half, width), bf16)],
            [smem] + [vmem] * (3 + count_exp),
            [vmem],
        )(starts, select, route_rows, whole, *pieces)[0]

    x_pieces = gathered(x_send)
    g_send = call(scaled_kernel, "scaled", send_shapes, [vmem] * (chips + 1), [vmem] * count_exp)(
        select, route_rows, *g_got
    )

    x_pieces[0] = after(x_pieces[0], g_send[0])
    x_mine = pack(False, tokens, x_pieces)
    x_other = core_swap(x_mine, count_fsdp)
    g_pieces = gathered(g_send)

    width_f = tile_of(hidden_local, 256)
    row_f = pl.BlockSpec((half, width_f), lambda i: (0, i))
    weight_f = pl.BlockSpec((1, width, width_f), lambda i: (0, 0, i))
    half_shape = ((half, hidden_local), bf16)
    h0, silu0, factor0, h1, silu1, factor1 = call(
        forward_kernel,
        "forward",
        [half_shape] * 6,
        [vmem, vmem, weight_f, weight_f],
        [row_f] * 6,
        grid=(hidden_local // width_f,),
        limit=54,
        flops=8 * half * width * hidden_local,
    )(x_mine, x_other, w_gate, w_up)

    g_pieces[0] = after(g_pieces[0], h0)
    grad_mine = pack(True, out_grad, g_pieces)
    grad_other = core_swap(grad_mine, count_fsdp)

    def backward(number, grad, silu, factor, *held):
        rows = pl.BlockSpec((half, width_f), lambda i: (number, i))
        return call(
            back_kernel,
            "backward",
            [((2 * half, hidden_local), bf16)] * 2,
            [vmem, pl.BlockSpec((1, width_f, width), lambda i: (0, i, 0)), row_f, row_f]
            + [pl.BlockSpec(memory_space=pl.ANY)] * len(held),
            [rows] * 2,
            grid=(hidden_local // width_f,),
        limit=14,
            alias={4: 0, 5: 1} if held else None,
        )(grad, w_down, silu, factor, *held)

    d_gate, d_up = backward(0, grad_mine, silu0, factor0)
    d_gate, d_up = backward(1, grad_other, silu1, factor1, d_gate, d_up)

    def part_of(h, d_gate, d_up):
        span = slice(h * count_exp * sub, (h + 1) * count_exp * sub)
        part = contract_last(d_gate, w_gate[0, span]) + contract_last(d_up, w_up[0, span])
        part = part.astype(bf16)
        return part, core_swap(part[half:], count_fsdp)

    def merge(part, from_core):
        outs = call(
            merge_kernel,
            "merge",
            [((half, sub), bf16)] * count_exp,
            [smem] + [vmem] * 2,
            [vmem] * count_exp,
        )(order * sub, part, from_core)
        return list(outs), gathered(outs)

    def to_tokens(came):
        own, *rest = call(
            token_kernel,
            "to_tokens",
            [((tok_count, sub), f32)] + [((tok_count, sub), bf16)] * (chips - 1),
            [vmem] * (1 + count_exp),
            [vmem] * chips,
        )(select, *came)
        return own, [chip_swap(rest[k - 1], k, count_fsdp) for k in steps]

    def summed(own, got):
        total = own
        for piece in got:
            total = total + piece.astype(f32)
        return gathered([total.astype(bf16)] * count_exp)

    parts = [part_of(h, d_gate, d_up) for h in range(parts_of_quarter)]
    all_came, sent = [], None
    for part, from_core in parts:
        sent, came = merge(part, from_core if sent is None else after(from_core, sent))
        all_came.append(came)
    proj_full = lax.all_gather(after(projection, g_got), "fsdp", axis=1, tiled=True)
    width_r = tile_of(rank, 256)
    low_spec = pl.BlockSpec((half, width_r), lambda i: (0, i))
    lows = call(
        low_kernel,
        "low",
        [((half, rank), bf16)] * 4,
        [vmem] * 4 + [pl.BlockSpec((width_r, width), lambda i: (i, 0))],
        [low_spec] * 4,
        grid=(rank // width_r,),
        limit=40,
    )(x_mine, x_other, grad_mine, grad_other, proj_full)
    all_came[0][0] = after(all_came[0][0], lows)
    across = pl.BlockSpec((1, rank, width_f), lambda i: (0, 0, i))
    along = pl.BlockSpec((1, width_f, rank), lambda i: (0, i, 0))
    both_f = pl.BlockSpec((2 * half, width_f), lambda i: (0, i))
    new_gate, new_up, new_down = call(
        momentum_kernel,
        "momentum",
        [(mom_gate.shape, f32), (mom_up.shape, f32), (mom_down.shape, f32)],
        [vmem] * 4 + [both_f] * 2 + [row_f] * 2 + [across, across, along],
        [across, across, along],
        grid=(hidden_local // width_f,),
        limit=20,
    )(*lows, d_gate, d_up, h0, h1, mom_gate, mom_up, mom_down)

    for came in all_came[1:]:
        came[0] = after(came[0], new_gate)
    totals = [to_tokens(came) for came in all_came]
    pieces = []
    for own, got in totals:
        pieces += summed(own, got)

    grad_tokens = call(
        place_kernel, "place", [((tok_count, width), bf16)], [smem] + [vmem] * len(pieces), [vmem]
    )(order * sub, *pieces)[0]
    return (grad_tokens, new_gate, new_up, new_down)


def solution(mesh):
    in_specs = (
        P("fsdp", None),
        P("fsdp", None),
        P("fsdp", None),
        P("fsdp", None),
        P("exp", None, "fsdp"),
        P("exp", None, "fsdp"),
        P("exp", "fsdp", None),
        P(None, "fsdp"),
        P("exp", None, "fsdp"),
        P("exp", None, "fsdp"),
        P("exp", "fsdp", None),
    )
    out_specs = (
        P("fsdp", None),
        P("exp", None, "fsdp"),
        P("exp", None, "fsdp"),
        P("exp", "fsdp", None),
    )
    return jax.shard_map(shards, mesh=mesh, in_specs=in_specs, out_specs=out_specs, check_vma=False)
```

```python
import functools

import jax
import jax.numpy as jnp
from jax import lax
from jax.experimental import pallas as pl
from jax.experimental.pallas import tpu as pltpu
from jax.sharding import PartitionSpec as P

momentum_decay = 0.9
grad_share = 0.1
lanes = 128
bf16 = jnp.bfloat16
f32 = jnp.float32
vmem = pl.BlockSpec(memory_space=pltpu.VMEM)
smem = pl.BlockSpec(memory_space=pltpu.SMEM)


def contract_last(left, right):
    return lax.dot_general(left, right, (((1,), (1,)), ((), ())), preferred_element_type=f32)


def contract_first(left, right):
    return lax.dot_general(left, right, (((0,), (0,)), ((), ())), preferred_element_type=f32)


def plain(left, right):
    return jnp.dot(left, right, preferred_element_type=f32)


def plane_swap(array, step, count):
    return lax.ppermute(array, "exp", [(i, i ^ step) for i in range(count)])


def core_swap(array, count):
    return lax.ppermute(array, "fsdp", [(i, i ^ 1) for i in range(count)])


def after(value, *others):
    return lax.optimization_barrier((value, others))[0]


def chip_swap(array, step, count):
    return lax.ppermute(array, "fsdp", [(i, i ^ (2 * step)) for i in range(count)])


def tile_of(size, wanted):
    return wanted if size % wanted == 0 else size


def routing_rows(experts_chosen, route_weight):
    rows = [experts_chosen.astype(f32).T]
    rest = route_weight.T
    for unused in range(3):
        term = lax.reduce_precision(rest, 8, 7)
        rows.append(term)
        rest = rest - term
    rows = jnp.concatenate(rows, axis=0)
    return jnp.pad(rows, ((0, -rows.shape[0] % 16), (0, 0))).astype(bf16)


def select_kernel(top, ids, own, *refs):
    experts = ids.shape[0]
    blocks = len(refs) - 1 - experts
    got, sends = refs[: blocks - 1], refs[blocks - 1 : blocks - 1 + experts]
    select, route_rows = refs[-2:]
    tok_count = own.shape[1]
    capacity = select.shape[1] // experts
    below = lax.broadcasted_iota(jnp.int32, (tok_count, tok_count), 0)
    right = lax.broadcasted_iota(jnp.int32, (tok_count, tok_count), 1)
    earlier = (below < right).astype(f32).astype(bf16)
    places = lax.broadcasted_iota(jnp.int32, (capacity, tok_count), 0).astype(f32)
    for k in range(blocks):
        rows = (own[...] if k == 0 else got[k - 1][tok_count : tok_count + own.shape[0], :tok_count]).astype(f32)
        chosen = rows[:top]
        weight = rows[top : 2 * top] + rows[2 * top : 3 * top] + rows[3 * top : 4 * top]
        members, routes = [], []
        for m in range(experts):
            hit = (chosen == ids[m].astype(f32)).astype(f32)
            members.append(jnp.max(hit, axis=0, keepdims=True))
            routes.append(jnp.sum(hit * weight, axis=0, keepdims=True))
        member = jnp.concatenate(members, axis=0)
        slot = plain(member.astype(bf16), earlier)
        for m in range(experts):
            here = (slot[m : m + 1] == places) & (member[m : m + 1] > 0.0)
            one = here.astype(f32)
            select[k, m * capacity : (m + 1) * capacity, :] = one.astype(bf16)
            share = jnp.sum(one * routes[m], axis=1, keepdims=True)
            route_rows[k, m * capacity : (m + 1) * capacity, :] = jnp.broadcast_to(
                share, (capacity, lanes)
            )
            if k:
                sends[m][(k - 1) * capacity : k * capacity, :] = plain(
                    one.astype(bf16), got[k - 1][:tok_count, :]
                ).astype(bf16)


def scaled_kernel(select, route_rows, *refs):
    blocks = select.shape[0]
    got, sends = refs[: blocks - 1], refs[blocks - 1 :]
    capacity = select.shape[1] // len(sends)
    for k in range(1, blocks):
        for m in range(len(sends)):
            span = slice(m * capacity, (m + 1) * capacity)
            rows = plain(select[k, span, :], got[k - 1][...]) * route_rows[k, span, :1]
            sends[m][(k - 1) * capacity : k * capacity, :] = rows.astype(bf16)


def pack_kernel(scale, starts, select, route_rows, whole, *refs):
    pieces, out = refs[:-1], refs[-1]
    experts = len(pieces)
    capacity = select.shape[1] // experts
    quarter = pieces[0].shape[1]
    own = plain(select[0, :capacity, :], whole[...])
    if scale:
        own = own * route_rows[0, :capacity, :1]
    out[:capacity, :] = own.astype(bf16)
    for m in range(experts):
        columns = pl.ds(pl.multiple_of(starts[m], lanes), quarter)
        out[capacity:, columns] = pieces[m][...]


def forward_kernel(mine, other, w_gate, w_up, *outs):
    for half, rows in enumerate((mine, other)):
        hidden, silu_out, factor_out = outs[3 * half : 3 * half + 3]
        gate = plain(rows[...], w_gate[0])
        up = plain(rows[...], w_up[0])
        sigma = jax.nn.sigmoid(gate)
        silu = gate * sigma
        hidden[...] = (silu * up).astype(bf16)
        silu_out[...] = silu.astype(bf16)
        factor_out[...] = (up * sigma * (1.0 + gate * (1.0 - sigma))).astype(bf16)


def back_kernel(grad, w_down, silu, factor, *refs):
    d_gate, d_up = refs[-2:]
    back = contract_last(grad[...], w_down[0])
    d_gate[...] = (back * factor[...].astype(f32)).astype(bf16)
    d_up[...] = (back * silu[...].astype(f32)).astype(bf16)


def merge_kernel(starts, part, more, *outs):
    half, sub = outs[0].shape
    for m, out in enumerate(outs):
        columns = pl.ds(pl.multiple_of(starts[m], lanes), sub)
        out[...] = (part[:half, columns].astype(f32) + more[:, columns].astype(f32)).astype(bf16)


def place_kernel(starts, *refs):
    pieces, out = refs[:-1], refs[-1]
    experts = starts.shape[0]
    sub = pieces[0].shape[1]
    for i, piece in enumerate(pieces):
        first = starts[i % experts] + (i // experts) * experts * sub
        out[:, pl.ds(pl.multiple_of(first, lanes), sub)] = piece[...]


def token_kernel(select, *refs):
    blocks = select.shape[0]
    came, outs = refs[:-blocks], refs[-blocks:]
    capacity = select.shape[1] // len(came)
    for k in range(blocks):
        rows = jnp.concatenate(
            [piece[k * capacity : (k + 1) * capacity, :] for piece in came], axis=0
        )
        outs[k][...] = contract_first(select[k], rows).astype(outs[k].dtype)


def low_kernel(mine, other, g_mine, g_other, projection, *outs):
    for rows, out in zip((mine, other, g_mine, g_other), outs):
        out[...] = contract_last(rows[...], projection[...]).astype(bf16)


def momentum_kernel(lt0, lt1, lg0, lg1, d_gate, d_up, h0, h1, mg, mu, md, og, ou, od):
    half = lt0.shape[0]
    for old, new, pairs in (
        (mg, og, ((lt0[...], d_gate[:half, :]), (lt1[...], d_gate[half:, :]))),
        (mu, ou, ((lt0[...], d_up[:half, :]), (lt1[...], d_up[half:, :]))),
        (md, od, ((h0[...], lg0[...]), (h1[...], lg1[...]))),
    ):
        total = contract_first(*pairs[0]) + contract_first(*pairs[1])
        new[0] = momentum_decay * old[0] + grad_share * total


def call(
    kernel, name, shapes, in_specs, out_specs, grid=(), scalars=0, limit=16, alias=None, flops=0
):
    return pl.pallas_call(
        kernel,
        name=name,
        out_shape=[jax.ShapeDtypeStruct(s, t) for s, t in shapes],
        grid_spec=pltpu.PrefetchScalarGridSpec(
            num_scalar_prefetch=scalars, grid=grid, in_specs=in_specs, out_specs=out_specs
        ),
        input_output_aliases=alias or {},
        compiler_params=pltpu.CompilerParams(vmem_limit_bytes=limit << 20),
        cost_estimate=pl.CostEstimate(flops=flops, bytes_accessed=0, transcendentals=0),
    )


def shards(
    tokens,
    out_grad,
    experts_chosen,
    route_weight,
    w_gate,
    w_up,
    w_down,
    projection,
    mom_gate,
    mom_up,
    mom_down,
):
    tok_count, width = tokens.shape
    top = experts_chosen.shape[1]
    hidden_local = w_gate.shape[2]
    rank = projection.shape[0]
    count_exp = lax.axis_size("exp")
    count_fsdp = lax.axis_size("fsdp")
    chips = count_fsdp // 2
    experts_all = count_exp * w_gate.shape[0]
    capacity = min(tok_count, tok_count * top * 5 // (4 * experts_all))
    capacity = -(-capacity // 16) * 16
    quarter = width // count_exp
    half = chips * capacity
    far = (chips - 1) * capacity
    expert = lax.axis_index("exp")
    steps = range(1, chips)
    order = expert ^ jnp.arange(count_exp, dtype=jnp.int32)
    starts = order * quarter

    own_routing = routing_rows(experts_chosen, route_weight)
    tall = own_routing.shape[0]
    start = expert * quarter
    x_part = jnp.concatenate(
        [
            lax.dynamic_slice_in_dim(tokens, start, quarter, 1),
            jnp.pad(own_routing, ((0, 0), (0, quarter - tok_count))),
        ],
        axis=0,
    )
    g_part = lax.dynamic_slice_in_dim(out_grad, start, quarter, 1)
    x_got = [chip_swap(x_part, k, count_fsdp) for k in steps]
    g_part = after(g_part, x_got)
    g_got = [chip_swap(g_part, k, count_fsdp) for k in steps]

    parts_of_quarter = next(n for n in (2, 3, 1) if quarter % (n * lanes) == 0 or n == 1)
    sub = quarter // parts_of_quarter

    send_shapes = [((far, quarter), bf16)] * count_exp
    *x_send, select, route_rows = call(
        functools.partial(select_kernel, top),
        "select",
        send_shapes
        + [
            ((chips, count_exp * capacity, tok_count), bf16),
            ((chips, count_exp * capacity, lanes), f32),
        ],
        [smem] + [vmem] * chips,
        [vmem] * (count_exp + 2),
    )(order, own_routing, *x_got)

    def gathered(send):
        return [send[0]] + [plane_swap(send[m], m, count_exp) for m in range(1, count_exp)]

    def pack(scale, whole, pieces):
        return call(
            functools.partial(pack_kernel, scale),
            "pack",
            [((half, width), bf16)],
            [smem] + [vmem] * (3 + count_exp),
            [vmem],
        )(starts, select, route_rows, whole, *pieces)[0]

    x_pieces = gathered(x_send)
    g_send = call(scaled_kernel, "scaled", send_shapes, [vmem] * (chips + 1), [vmem] * count_exp)(
        select, route_rows, *g_got
    )

    x_pieces[0] = after(x_pieces[0], g_send[0])
    x_mine = pack(False, tokens, x_pieces)
    x_other = core_swap(x_mine, count_fsdp)
    g_pieces = gathered(g_send)

    width_f = tile_of(hidden_local, 256)
    row_f = pl.BlockSpec((half, width_f), lambda i: (0, i))
    weight_f = pl.BlockSpec((1, width, width_f), lambda i: (0, 0, i))
    half_shape = ((half, hidden_local), bf16)
    h0, silu0, factor0, h1, silu1, factor1 = call(
        forward_kernel,
        "forward",
        [half_shape] * 6,
        [vmem, vmem, weight_f, weight_f],
        [row_f] * 6,
        grid=(hidden_local // width_f,),
        limit=54,
        flops=8 * half * width * hidden_local,
    )(x_mine, x_other, w_gate, w_up)

    g_pieces[0] = after(g_pieces[0], h0)
    grad_mine = pack(True, out_grad, g_pieces)
    grad_other = core_swap(grad_mine, count_fsdp)

    def backward(number, grad, silu, factor, *held):
        width_b = tile_of(hidden_local, 512)
        rows = pl.BlockSpec((half, width_b), lambda i: (number, i))
        row_b = pl.BlockSpec((half, width_b), lambda i: (0, i))
        return call(
            back_kernel,
            "backward",
            [((2 * half, hidden_local), bf16)] * 2,
            [vmem, pl.BlockSpec((1, width_b, width), lambda i: (0, i, 0)), row_b, row_b]
            + [pl.BlockSpec(memory_space=pl.ANY)] * len(held),
            [rows] * 2,
            grid=(hidden_local // width_b,),
        limit=20,
            alias={4: 0, 5: 1} if held else None,
        )(grad, w_down, silu, factor, *held)

    d_gate, d_up = backward(0, grad_mine, silu0, factor0)
    d_gate, d_up = backward(1, grad_other, silu1, factor1, d_gate, d_up)

    def part_of(h, d_gate, d_up):
        span = slice(h * count_exp * sub, (h + 1) * count_exp * sub)
        part = contract_last(d_gate, w_gate[0, span]) + contract_last(d_up, w_up[0, span])
        part = part.astype(bf16)
        return part, core_swap(part[half:], count_fsdp)

    def merge(part, from_core):
        outs = call(
            merge_kernel,
            "merge",
            [((half, sub), bf16)] * count_exp,
            [smem] + [vmem] * 2,
            [vmem] * count_exp,
        )(order * sub, part, from_core)
        return list(outs), gathered(outs)

    def to_tokens(came):
        own, *rest = call(
            token_kernel,
            "to_tokens",
            [((tok_count, sub), f32)] + [((tok_count, sub), bf16)] * (chips - 1),
            [vmem] * (1 + count_exp),
            [vmem] * chips,
        )(select, *came)
        return own, [chip_swap(rest[k - 1], k, count_fsdp) for k in steps]

    def summed(own, got):
        total = own
        for piece in got:
            total = total + piece.astype(f32)
        return gathered([total.astype(bf16)] * count_exp)

    parts = [part_of(h, d_gate, d_up) for h in range(parts_of_quarter)]
    all_came, sent = [], None
    for part, from_core in parts:
        sent, came = merge(part, from_core if sent is None else after(from_core, sent))
        all_came.append(came)
    proj_full = lax.all_gather(after(projection, g_got), "fsdp", axis=1, tiled=True)
    width_r = tile_of(rank, 256)
    low_spec = pl.BlockSpec((half, width_r), lambda i: (0, i))
    lows = call(
        low_kernel,
        "low",
        [((half, rank), bf16)] * 4,
        [vmem] * 4 + [pl.BlockSpec((width_r, width), lambda i: (i, 0))],
        [low_spec] * 4,
        grid=(rank // width_r,),
        limit=40,
    )(x_mine, x_other, grad_mine, grad_other, proj_full)
    all_came[0][0] = after(all_came[0][0], lows)
    across = pl.BlockSpec((1, rank, width_f), lambda i: (0, 0, i))
    along = pl.BlockSpec((1, width_f, rank), lambda i: (0, i, 0))
    both_f = pl.BlockSpec((2 * half, width_f), lambda i: (0, i))
    new_gate, new_up, new_down = call(
        momentum_kernel,
        "momentum",
        [(mom_gate.shape, f32), (mom_up.shape, f32), (mom_down.shape, f32)],
        [vmem] * 4 + [both_f] * 2 + [row_f] * 2 + [across, across, along],
        [across, across, along],
        grid=(hidden_local // width_f,),
        limit=20,
    )(*lows, d_gate, d_up, h0, h1, mom_gate, mom_up, mom_down)

    for came in all_came[1:]:
        came[0] = after(came[0], new_gate)
    totals = [to_tokens(came) for came in all_came]
    pieces = []
    for own, got in totals:
        pieces += summed(own, got)

    grad_tokens = call(
        place_kernel, "place", [((tok_count, width), bf16)], [smem] + [vmem] * len(pieces), [vmem]
    )(order * sub, *pieces)[0]
    return (grad_tokens, new_gate, new_up, new_down)


def solution(mesh):
    in_specs = (
        P("fsdp", None),
        P("fsdp", None),
        P("fsdp", None),
        P("fsdp", None),
        P("exp", None, "fsdp"),
        P("exp", None, "fsdp"),
        P("exp", "fsdp", None),
        P(None, "fsdp"),
        P("exp", None, "fsdp"),
        P("exp", None, "fsdp"),
        P("exp", "fsdp", None),
    )
    out_specs = (
        P("fsdp", None),
        P("exp", None, "fsdp"),
        P("exp", None, "fsdp"),
        P("exp", "fsdp", None),
    )
    return jax.shard_map(shards, mesh=mesh, in_specs=in_specs, out_specs=out_specs, check_vma=False)
```
